32 devices in a mesh: replica: 8 (over z, core), shard: 4 (over y, x).
Axes of the slice: x: 2, y: 2, z: 4, core: 2. Of those that a mesh axis runs over, the one named last changes fastest.
Arguments:
- tokens: bfloat16 [32, 864, 1024], P('replica', 'shard'), may hold values from -6 to 6
- counts: int32 [32, 4], P('replica'), may hold values from 1 to 216, 577 in all within a row
- w_qkv: bfloat16 [1024, 3072], P('shard'), may hold values from -0.1875 to 0.1875
- w_proj: bfloat16 [1024, 1024], P('shard'), may hold values from -0.5 to 0.5
- w_fc1: bfloat16 [1024, 4096], P('shard'), may hold values from -0.1875 to 0.1875
- w_fc2: bfloat16 [4096, 1024], P('shard'), may hold values from -0.09375 to 0.09375
- norm_gains: bfloat16 [2048], P('shard'), may hold values from 0.25 to 1.75
- biases: bfloat16 [10240], P('shard'), may hold values from -3 to 3
- grad_out: bfloat16 [32, 864, 1024], P('replica', 'shard'), may hold values from -6 to 6
Outputs:
- result: bfloat16 [32, 864, 1024], P('replica', 'shard')
- grad_tokens: float32 [32, 864, 1024], P('replica', 'shard')
- grad_w_qkv: float32 [1024, 3072], P('shard')
- grad_w_proj: float32 [1024, 1024], P('shard')
- grad_w_fc1: float32 [1024, 4096], P('shard')
- grad_w_fc2: float32 [4096, 1024], P('shard')
- grad_norm_gains: float32 [2048], P('shard')
- grad_biases: float32 [10240], P('shard')
The draws below stay inside these ranges and needn't reach their ends.
Inputs may be any that keep to these rules, and one draw needn't show every extreme that they name: valid rows of each image on each device of the shard axis, the first ones of its 216 slots there; an image's counts sum to 577; in every draw some image has 216 valid rows on some device.
All inputs are finite; a program needn't handle non-finite values.
Results may differ from the reference program's by a relative error of at most 0.0079.
Values may be sent and summed in bfloat16 or wider, within the bound.
A program may use at most 320 MiB of HBM per device.

```python
import math
import jax
import jax.numpy as jnp
import numpy as np
from jax import lax

D = 1024
HEADS = 16
HEAD = 64
FF = 4096
LEN = 577
IMG_UNIT = 1
IMAGES = 32
SLOT = 216
N_REPLICA = 8
N_SHARD = 4


def shard_levels(key, extent, shards, low, high):
    loudness, own = 1.0, jax.random.fold_in(key, 6)
    for dim, parts in shards:
        draws = jnp.exp(jax.random.uniform(jax.random.fold_in(own, dim), (parts,), jnp.float32, low / len(shards), high / len(shards)))
        loudness = loudness * jnp.repeat(draws, extent[dim] // parts).reshape([-1 if axis == dim else 1 for axis in range(len(extent))])
    return loudness


def split_up(count, total, limit, lean):
    weights = [(1 << 20) // math.isqrt(standing ** lean) + 1 for standing in range(2, count + 1)]
    surplus, given = total - limit - (count - 1), [1] * (count - 1)
    while surplus > 0:
        free = [i for i in range(count - 1) if given[i] < limit]
        whole, left = sum([weights[i] for i in free]), surplus
        for i in free:
            addition = min(limit - given[i], max(1, left * weights[i] // whole), surplus)
            given[i] = given[i] + addition
            surplus = surplus - addition
    return np.array([limit] + given)


def ragged_sizes(stream_key, amount, total, bound, skew):
    if amount == 2:
        one = jax.random.randint(stream_key, (), max(1, total - bound), min(bound, total - 1) + 1)
        return jnp.stack([one, total - one])
    tallies = jnp.asarray(split_up(amount, total, bound, skew), jnp.int32)
    pairs = (amount - 1) // 2
    giver, sink = tallies[1:1 + 2 * pairs:2], tallies[2:2 + 2 * pairs:2]
    slack = jnp.minimum(giver - 1, bound - sink)
    passed = jax.random.randint(jax.random.fold_in(stream_key, 1), (pairs,), 0, 1 << 20) % (slack + 1)
    tallies = tallies.at[1:1 + 2 * pairs:2].set(giver - passed).at[2:2 + 2 * pairs:2].set(sink + passed)
    return tallies[jax.random.permutation(jax.random.fold_in(stream_key, 2), amount)]


def bell_draw(own_key, dims, deviation, reach, shards=(), held_as=jnp.bfloat16):
    array = deviation * jax.random.normal(own_key, dims, jnp.float32)
    if shards:
        array = array * shard_levels(own_key, dims, shards, -0.22, 0.18)
    return jnp.clip(array, -reach, reach).astype(held_as)


def setup_inputs(seed: int = 0) -> dict:
    streams_of = jax.random.split(jax.random.key(seed), 10)
    return {
        "tokens": bell_draw(streams_of[0], (IMAGES, N_SHARD * SLOT, D), 1.0, 6.0, ((0, 8), (1, 4))),
        "counts": jax.vmap(lambda own: ragged_sizes(own, N_SHARD, LEN, SLOT, 2))(jax.random.split(streams_of[1], IMAGES)).reshape((IMAGES, N_SHARD)).astype(jnp.int32),
        "w_qkv": bell_draw(streams_of[2], (D, 3 * D), D ** -0.5, 0.1875, ((0, 4),)),
        "w_proj": bell_draw(streams_of[3], (D, D), (D // 8) ** -0.5, 0.5, ((0, 4),)),
        "w_fc1": bell_draw(streams_of[4], (D, FF), D ** -0.5, 0.1875, ((0, 4),)),
        "w_fc2": bell_draw(streams_of[5], (FF, D), FF ** -0.5, 0.09375, ((0, 4),)),
        "norm_gains": jnp.clip(1.0 + 0.15 * jax.random.normal(streams_of[6], (2 * D,), jnp.float32), 0.25, 1.75).astype(jnp.bfloat16),
        "biases": bell_draw(streams_of[7], (6 * D + FF,), 0.5, 3.0, ((0, 4),)),
        "grad_out": bell_draw(streams_of[8], (IMAGES, N_SHARD * SLOT, D), 1.0, 6.0, ((0, 8), (1, 4))),
    }


@jax.custom_vjp
def low(v):
    return lax.optimization_barrier(v.astype(jnp.bfloat16)).astype(jnp.float32)

@jax.custom_vjp
def low_back(v):
    return v

def low_keep(v):
    return (low(v), None)

def low_pass(kept, grad):
    return (grad,)

def back_keep(v):
    return (v, None)

def back_low(kept, grad):
    return (low(grad),)
low.defvjp(low_keep, low_pass)
low_back.defvjp(back_keep, back_low)
norm_eps = 1e-06
big_negative = -1e+30

def highest(left, right):
    return jnp.dot(left, right, precision=lax.Precision.HIGHEST, preferred_element_type=jnp.float32)

def layer_norm(values, norm_gain, norm_shift):
    centered = values - lax.optimization_barrier(jnp.mean(values, axis=-1, keepdims=True))
    spread = lax.optimization_barrier(jnp.mean(centered * centered, axis=-1, keepdims=True))
    return centered * lax.rsqrt(spread + norm_eps) * norm_gain + norm_shift

def group_forward(params, inputs, valid_rows):
    w_qkv, w_proj, w_fc1, w_fc2, norm_gains, biases = params
    image_count = inputs.shape[0]
    image_rows = inputs.shape[1]
    flat_rows = inputs.reshape(-1, D)
    normed_one = low(layer_norm(flat_rows, norm_gains[:D], biases[:D]))
    mixed_rows = highest(normed_one, w_qkv)
    queries = low(low_back(mixed_rows[:, :D] + biases[2 * D:3 * D]))
    key_rows = low(low_back(mixed_rows[:, D:2 * D]))
    value_rows = low(low_back(mixed_rows[:, 2 * D:] + biases[3 * D:4 * D]))
    head_shape = (image_count, image_rows, HEADS, HEAD)
    scores = jnp.einsum('bqhe,bkhe->bhqk', queries.reshape(head_shape), key_rows.reshape(head_shape), precision=lax.Precision.HIGHEST, preferred_element_type=jnp.float32) * HEAD ** (-0.5)
    scores = jnp.where(valid_rows[:, None, None, :] > 0.5, scores, big_negative)
    scores = low_back(scores)
    attn_probs = low(jax.nn.softmax(scores, axis=-1))
    attended = jnp.einsum('bhqk,bkhe->bqhe', attn_probs, value_rows.reshape(head_shape), precision=lax.Precision.HIGHEST, preferred_element_type=jnp.float32)
    attended = low(low_back(attended.reshape(-1, D)))
    branch_one = low_back(highest(attended, w_proj) + biases[4 * D:5 * D])
    middle = flat_rows + branch_one
    normed_two = low(layer_norm(middle, norm_gains[D:], biases[D:2 * D]))
    before = low_back(highest(normed_two, w_fc1) + biases[6 * D:])
    hidden = low(jax.nn.gelu(before, approximate=False))
    branch_two = low_back(highest(hidden, w_fc2) + biases[5 * D:6 * D])
    outcome = (middle + branch_two) * valid_rows.reshape(-1, 1)
    return outcome.reshape(inputs.shape)

def reference(tokens, counts, w_qkv, w_proj, w_fc1, w_fc2, norm_gains, biases, grad_out):
    rows_index = jnp.arange(N_SHARD * SLOT, dtype=jnp.int32)
    owners = rows_index // SLOT
    valid_rows = ((rows_index % SLOT)[None, :] < counts[:, owners]).astype(jnp.float32)
    group_shape = (N_REPLICA, IMG_UNIT * N_SHARD, N_SHARD * SLOT, D)
    inputs = tokens.astype(jnp.float32).reshape(group_shape)
    valid_groups = valid_rows.reshape(group_shape[:3])
    params = tuple((member.astype(jnp.float32) for member in (w_qkv, w_proj, w_fc1, w_fc2, norm_gains, biases)))
    group_step = jax.checkpoint(group_forward)

    def forward(params_now, inputs_now):
        return lax.map(lambda members: group_step(params_now, members[0], members[1]), (inputs_now, valid_groups))
    outputs, pullback = jax.vjp(forward, params, inputs)
    grad_params, grad_inputs = pullback(grad_out.astype(jnp.float32).reshape(group_shape))
    out_shape = tokens.shape
    return (outputs.reshape(out_shape).astype(jnp.bfloat16), grad_inputs.reshape(out_shape), grad_params[0], grad_params[1], grad_params[2], grad_params[3], grad_params[4], grad_params[5])
```

```python
import functools

import jax
import jax.numpy as jnp
from jax import lax
from jax.experimental import pallas as pl
from jax.experimental.pallas import tpu as pltpu
from jax.sharding import Mesh, PartitionSpec as P

HEAD = 64
LANES = 2 * HEAD
SCALE = HEAD ** (-0.5)

norm_eps = 1e-06
big_negative = -1e30
BF = jnp.bfloat16
F32 = jnp.float32
SWAP = [(0, 1), (1, 0)]


def layer_norm(values, norm_gain, norm_shift):
    centered = values - jnp.mean(values, axis=-1, keepdims=True)
    spread = jnp.mean(centered * centered, axis=-1, keepdims=True)
    return centered * lax.rsqrt(spread + norm_eps) * norm_gain + norm_shift


def exact_gelu(values):
    return jax.nn.gelu(values, approximate=False)


def rows_inner(left, right):
    return lax.dot_general(left, right, (((0,), (0,)), ((), ())), preferred_element_type=F32)


def times_transpose(left, right):
    return lax.dot_general(left, right, (((1,), (1,)), ((), ())), preferred_element_type=F32)


def times(left, right):
    return jnp.dot(left, right, preferred_element_type=F32)


def softmax_parts(query, mixed_ref, key_masks, sources):
    scores = []
    for b in range(sources):
        key_rows = mixed_ref[b, 0, :, LANES : 2 * LANES]
        scores.append(jnp.where(key_masks[b], times_transpose(query, key_rows) * SCALE, big_negative))
    row_max = functools.reduce(
        jnp.maximum, [jnp.max(part, axis=1, keepdims=True) for part in scores]
    )
    exps = [jnp.exp(part - row_max) for part in scores]
    total = functools.reduce(jnp.add, [jnp.sum(part, axis=1, keepdims=True) for part in exps])
    return exps, 1.0 / total


def masks_of(counts_ref, image, sources, slot):
    column = lax.broadcasted_iota(jnp.int32, (1, slot), 1)
    return [column < counts_ref[image, b] for b in range(sources)]


def forward_kernel(counts_ref, mixed_ref, attended_ref):
    sources, slot = mixed_ref.shape[0], mixed_ref.shape[2]
    key_masks = masks_of(counts_ref, pl.program_id(0), sources, slot)
    low_lanes = lax.broadcasted_iota(jnp.int32, (1, LANES), 1) < HEAD

    def one_source(a, carry):
        query = mixed_ref[a, 0, :, 0:LANES]
        outs = []
        for head in range(2):
            kept = low_lanes if head == 0 else jnp.logical_not(low_lanes)
            own = jnp.where(kept, query, jnp.zeros_like(query))
            exps, inverse = softmax_parts(own, mixed_ref, key_masks, sources)
            out = None
            for b in range(sources):
                probs = (exps[b] * inverse).astype(BF)
                term = times(probs, mixed_ref[b, 0, :, 2 * LANES : 3 * LANES])
                out = term if out is None else out + term
            outs.append(out)
        attended_ref[a, 0] = jnp.where(low_lanes, outs[0], outs[1]).astype(BF)
        return carry

    lax.fori_loop(0, sources, one_source, 0)


def backward_kernel(counts_ref, mixed_ref, grad_ref, out_ref, key_sum, value_sum):
    sources, slot = mixed_ref.shape[0], mixed_ref.shape[2]
    key_masks = masks_of(counts_ref, pl.program_id(0), sources, slot)
    low_lanes = lax.broadcasted_iota(jnp.int32, (1, LANES), 1) < HEAD
    key_sum[...] = jnp.zeros_like(key_sum)
    value_sum[...] = jnp.zeros_like(value_sum)

    def one_source(a, carry):
        query = mixed_ref[a, 0, :, 0:LANES]
        grad = grad_ref[a, 0]
        outs = []
        for head in range(2):
            kept = low_lanes if head == 0 else jnp.logical_not(low_lanes)
            own = jnp.where(kept, query, jnp.zeros_like(query))
            own_grad = jnp.where(kept, grad, jnp.zeros_like(grad))
            exps, inverse = softmax_parts(own, mixed_ref, key_masks, sources)
            probs, grad_probs, inner = [], [], None
            for b in range(sources):
                part = exps[b] * inverse
                grad_part = times_transpose(own_grad, mixed_ref[b, 0, :, 2 * LANES : 3 * LANES])
                term = jnp.sum(part * grad_part, axis=1, keepdims=True)
                inner = term if inner is None else inner + term
                probs.append(part)
                grad_probs.append(grad_part)
                value_sum[b] += rows_inner(part.astype(BF), own_grad)
            out = None
            for b in range(sources):
                grad_scores = (probs[b] * (grad_probs[b] - inner)).astype(BF)
                term = times(grad_scores, mixed_ref[b, 0, :, LANES : 2 * LANES])
                out = term if out is None else out + term
                key_sum[b] += rows_inner(grad_scores, own)
            outs.append(out)
        out_ref[a, 0, :, 0:LANES] = (jnp.where(low_lanes, outs[0], outs[1]) * SCALE).astype(BF)
        return carry

    lax.fori_loop(0, sources, one_source, 0)
    for b in range(sources):
        out_ref[b, 0, :, LANES : 2 * LANES] = (key_sum[b] * SCALE).astype(BF)
        out_ref[b, 0, :, 2 * LANES : 3 * LANES] = value_sum[b].astype(BF)


def attention_specs(sources, slot, width):
    return pl.BlockSpec((sources, 1, slot, width), lambda i, p: (0, i, 0, p))


def attend_forward(counts, mixed):
    sources, images, slot, width = mixed.shape
    pairs = width // (3 * LANES)
    work = 4 * images * pairs * (sources * slot) ** 2 * LANES
    return pl.pallas_call(
        forward_kernel,
        grid=(images, pairs),
        in_specs=[
            pl.BlockSpec(memory_space=pltpu.SMEM),
            attention_specs(sources, slot, 3 * LANES),
        ],
        out_specs=attention_specs(sources, slot, LANES),
        out_shape=jax.ShapeDtypeStruct((sources, images, slot, pairs * LANES), BF),
        compiler_params=pltpu.CompilerParams(vmem_limit_bytes=40 * 2**20),
        cost_estimate=pl.CostEstimate(flops=work, bytes_accessed=mixed.size * 3, transcendentals=0),
    )(counts, mixed)


def attend_backward(counts, mixed, grad_attended):
    sources, images, slot, width = mixed.shape
    pairs = width // (3 * LANES)
    work = 10 * images * pairs * (sources * slot) ** 2 * LANES
    return pl.pallas_call(
        backward_kernel,
        grid=(images, pairs),
        in_specs=[
            pl.BlockSpec(memory_space=pltpu.SMEM),
            attention_specs(sources, slot, 3 * LANES),
            attention_specs(sources, slot, LANES),
        ],
        out_specs=attention_specs(sources, slot, 3 * LANES),
        out_shape=jax.ShapeDtypeStruct(mixed.shape, BF),
        scratch_shapes=[
            pltpu.VMEM((sources, slot, LANES), F32),
            pltpu.VMEM((sources, slot, LANES), F32),
        ],
        compiler_params=pltpu.CompilerParams(vmem_limit_bytes=40 * 2**20),
        cost_estimate=pl.CostEstimate(flops=work, bytes_accessed=mixed.size * 5, transcendentals=0),
    )(counts, mixed, grad_attended)


def reduce_weight(grad, shards):
    rows, columns = grad.shape
    core = lax.axis_index("core")
    halves = grad.reshape(shards, 2, rows // shards // 2, columns)
    own = lax.dynamic_index_in_dim(halves, core, 1, keepdims=False)
    other = lax.dynamic_index_in_dim(halves, 1 - core, 1, keepdims=False).astype(BF)
    received = lax.ppermute(other, "core", SWAP)
    chip = (own + received.astype(F32)).astype(BF).reshape(rows // 2, columns)
    group = lax.psum_scatter(chip, "shard", scatter_dimension=0, tiled=True)
    total = lax.psum(group, "rep")
    partner = lax.ppermute(total, "core", SWAP)
    pair = jnp.stack([jnp.where(core == 0, total, partner), jnp.where(core == 0, partner, total)])
    return pair.reshape(rows // shards, columns).astype(F32)


def per_device(tokens, counts, w_qkv, w_proj, w_fc1, w_fc2, norm_gains, biases, grad_out):
    images, slot_rows, width = tokens.shape
    shards = lax.axis_size("shard")
    shard_rank = lax.axis_index("shard")
    row_count = images * slot_rows
    shaped = (images, slot_rows, width)
    pairs = width // LANES
    own_counts = lax.dynamic_slice_in_dim(counts, shard_rank, 1, 1)
    slot_index = jnp.arange(slot_rows, dtype=jnp.int32)
    row_valid = (slot_index[None, :] < own_counts).astype(F32).reshape(row_count, 1)

    qkv_paired = w_qkv.reshape(-1, 3, pairs, LANES).swapaxes(1, 2).reshape(w_qkv.shape)
    vectors = lax.all_gather(jnp.concatenate([norm_gains, biases]), "shard", axis=0, tiled=False)
    gain_len = norm_gains.shape[0]
    gains_wide = vectors[:, :gain_len].reshape(-1).astype(F32)
    biases_wide = vectors[:, gain_len:].reshape(-1).astype(F32)
    qkv_full = lax.all_gather(qkv_paired, "shard", axis=0, tiled=True)
    proj_full = lax.all_gather(w_proj, "shard", axis=0, tiled=True)
    fc1_full = lax.all_gather(w_fc1, "shard", axis=0, tiled=True)
    fc2_full = lax.all_gather(w_fc2, "shard", axis=0, tiled=True)

    inputs = tokens.astype(F32).reshape(row_count, width)
    normed_wide, norm_one_back = jax.vjp(
        layer_norm, inputs, gains_wide[:width], biases_wide[:width]
    )
    normed_one = normed_wide.astype(BF)
    query_bias = biases_wide[2 * width : 3 * width].reshape(pairs, 1, LANES)
    value_bias = biases_wide[3 * width : 4 * width].reshape(pairs, 1, LANES)
    mixed_bias = jnp.concatenate([query_bias, jnp.zeros_like(query_bias), value_bias], axis=1)
    mixed = (times(normed_one, qkv_full) + mixed_bias.reshape(1, 3 * width)).astype(BF)
    own_heads = lax.all_to_all(
        mixed.reshape(row_count, shards, -1), "shard", split_axis=1, concat_axis=0
    )
    own_heads = own_heads.reshape(shards, images, slot_rows, -1)
    attended = attend_forward(counts, own_heads)
    attended = lax.all_to_all(
        attended.reshape(shards, row_count, -1), "shard", split_axis=0, concat_axis=1
    ).reshape(row_count, width)
    middle = inputs + times(attended, proj_full) + biases_wide[4 * width : 5 * width]
    normed_mid, norm_two_back = jax.vjp(
        layer_norm, middle, gains_wide[width:], biases_wide[width : 2 * width]
    )
    normed_two = normed_mid.astype(BF)
    before = times(normed_two, fc1_full) + biases_wide[6 * width :]
    hidden_wide, gelu_back = jax.vjp(exact_gelu, before)
    hidden = hidden_wide.astype(BF)
    outcome = (middle + times(hidden, fc2_full) + biases_wide[5 * width : 6 * width]) * row_valid
    output = outcome.astype(BF).reshape(shaped)

    grad_rows = grad_out.astype(F32).reshape(row_count, width) * row_valid
    grad_branch = grad_rows.astype(BF)
    grad_fc2 = reduce_weight(rows_inner(hidden, grad_branch), shards)
    grad_out_bias = jnp.sum(grad_branch, axis=0, dtype=F32)
    grad_hidden = times_transpose(grad_branch, fc2_full)
    grad_before = gelu_back(grad_hidden)[0].astype(BF)
    grad_fc1 = reduce_weight(rows_inner(normed_two, grad_before), shards)
    grad_hidden_bias = jnp.sum(grad_before, axis=0, dtype=F32)
    grad_normed_two = times_transpose(grad_before, fc1_full)
    grad_middle_norm, grad_gain_two, grad_shift_two = norm_two_back(grad_normed_two)
    grad_middle = grad_rows + grad_middle_norm
    grad_branch_one = grad_middle.astype(BF)
    grad_proj = reduce_weight(rows_inner(attended, grad_branch_one), shards)
    grad_proj_bias = jnp.sum(grad_branch_one, axis=0, dtype=F32)
    grad_attended = times_transpose(grad_branch_one, proj_full).astype(BF)
    grad_heads = lax.all_to_all(
        grad_attended.reshape(row_count, shards, -1), "shard", split_axis=1, concat_axis=0
    ).reshape(shards, images, slot_rows, -1)
    grad_own = attend_backward(counts, own_heads, grad_heads)
    grad_mixed = lax.all_to_all(
        grad_own.reshape(shards, row_count, -1), "shard", split_axis=0, concat_axis=1
    ).reshape(row_count, 3 * width)
    grad_qkv = reduce_weight(rows_inner(normed_one, grad_mixed), shards)
    grad_qkv = grad_qkv.reshape(-1, pairs, 3, LANES).swapaxes(1, 2).reshape(w_qkv.shape)
    column_sums = jnp.sum(grad_mixed, axis=0, dtype=F32).reshape(pairs, 3, LANES)
    grad_normed_one = times_transpose(grad_mixed, qkv_full)
    grad_inputs_norm, grad_gain_one, grad_shift_one = norm_one_back(grad_normed_one)
    grad_tokens = (grad_middle + grad_inputs_norm).reshape(shaped)
    grad_gains = jnp.concatenate([grad_gain_one, grad_gain_two]).reshape(shards, -1)
    grad_biases = jnp.concatenate(
        [
            grad_shift_one,
            grad_shift_two,
            column_sums[:, 0].reshape(-1),
            column_sums[:, 2].reshape(-1),
            grad_proj_bias,
            grad_out_bias,
            grad_hidden_bias,
        ]
    ).reshape(shards, -1)
    grad_vectors = lax.psum(
        jnp.concatenate([grad_gains, grad_biases], axis=1), ("rep", "core", "shard")
    )
    own_vectors = lax.dynamic_index_in_dim(grad_vectors, shard_rank, 0, keepdims=False)
    return (
        output,
        grad_tokens,
        grad_qkv,
        grad_proj,
        grad_fc1,
        grad_fc2,
        own_vectors[:gain_len],
        own_vectors[gain_len:],
    )


def solution(mesh):
    replicas, shards = mesh.devices.shape
    split = Mesh(mesh.devices.reshape(replicas // 2, 2, shards), ("rep", "core", "shard"))
    both = ("rep", "core")
    rows, weight, vector = P(both, "shard", None), P("shard", None), P("shard")
    in_specs = (rows, P(both, None)) + (weight,) * 4 + (vector,) * 2 + (rows,)
    out_specs = (rows, rows) + (weight,) * 4 + (vector,) * 2
    return jax.shard_map(
        per_device, mesh=split, in_specs=in_specs, out_specs=out_specs, check_vma=False
    )
```

```python
import functools

import jax
import jax.numpy as jnp
from jax import lax
from jax.experimental import pallas as pl
from jax.experimental.pallas import tpu as pltpu
from jax.sharding import Mesh, PartitionSpec as P

HEAD = 64
LANES = 2 * HEAD
SCALE = HEAD ** (-0.5)

norm_eps = 1e-06
big_negative = -1e30
BF = jnp.bfloat16
F32 = jnp.float32
SWAP = [(0, 1), (1, 0)]


def layer_norm(values, norm_gain, norm_shift):
    centered = values - jnp.mean(values, axis=-1, keepdims=True)
    spread = jnp.mean(centered * centered, axis=-1, keepdims=True)
    return centered * lax.rsqrt(spread + norm_eps) * norm_gain + norm_shift


def rows_inner(left, right):
    return lax.dot_general(left, right, (((0,), (0,)), ((), ())), preferred_element_type=F32)


def times_transpose(left, right):
    return lax.dot_general(left, right, (((1,), (1,)), ((), ())), preferred_element_type=F32)


def times(left, right):
    return jnp.dot(left, right, preferred_element_type=F32)


def softmax_parts(query, mixed_ref, key_masks, sources):
    scores = []
    for b in range(sources):
        key_rows = mixed_ref[b, 0, :, LANES : 2 * LANES]
        scores.append(jnp.where(key_masks[b], times_transpose(query, key_rows) * SCALE, big_negative))
    row_max = functools.reduce(
        jnp.maximum, [jnp.max(part, axis=1, keepdims=True) for part in scores]
    )
    exps = [jnp.exp(part - row_max) for part in scores]
    total = functools.reduce(jnp.add, [jnp.sum(part, axis=1, keepdims=True) for part in exps])
    return exps, 1.0 / total


def masks_of(counts_ref, image, sources, slot):
    column = lax.broadcasted_iota(jnp.int32, (1, slot), 1)
    return [column < counts_ref[image, b] for b in range(sources)]


def forward_kernel(counts_ref, mixed_ref, attended_ref):
    sources, slot = mixed_ref.shape[0], mixed_ref.shape[2]
    key_masks = masks_of(counts_ref, pl.program_id(0), sources, slot)
    low_lanes = lax.broadcasted_iota(jnp.int32, (1, LANES), 1) < HEAD

    def one_source(a, carry):
        query = mixed_ref[a, 0, :, 0:LANES]
        outs = []
        for head in range(2):
            kept = low_lanes if head == 0 else jnp.logical_not(low_lanes)
            own = jnp.where(kept, query, jnp.zeros_like(query))
            exps, inverse = softmax_parts(own, mixed_ref, key_masks, sources)
            out = None
            for b in range(sources):
                probs = (exps[b] * inverse).astype(BF)
                term = times(probs, mixed_ref[b, 0, :, 2 * LANES : 3 * LANES])
                out = term if out is None else out + term
            outs.append(out)
        attended_ref[a, 0] = jnp.where(low_lanes, outs[0], outs[1]).astype(BF)
        return carry

    lax.fori_loop(0, sources, one_source, 0)


def backward_kernel(counts_ref, mixed_ref, grad_ref, out_ref, key_sum, value_sum):
    sources, slot = mixed_ref.shape[0], mixed_ref.shape[2]
    key_masks = masks_of(counts_ref, pl.program_id(0), sources, slot)
    low_lanes = lax.broadcasted_iota(jnp.int32, (1, LANES), 1) < HEAD
    key_sum[...] = jnp.zeros_like(key_sum)
    value_sum[...] = jnp.zeros_like(value_sum)

    def one_source(a, carry):
        query = mixed_ref[a, 0, :, 0:LANES]
        grad = grad_ref[a, 0]
        outs = []
        for head in range(2):
            kept = low_lanes if head == 0 else jnp.logical_not(low_lanes)
            own = jnp.where(kept, query, jnp.zeros_like(query))
            own_grad = jnp.where(kept, grad, jnp.zeros_like(grad))
            exps, inverse = softmax_parts(own, mixed_ref, key_masks, sources)
            probs, grad_probs, inner = [], [], None
            for b in range(sources):
                part = exps[b] * inverse
                grad_part = times_transpose(own_grad, mixed_ref[b, 0, :, 2 * LANES : 3 * LANES])
                term = jnp.sum(part * grad_part, axis=1, keepdims=True)
                inner = term if inner is None else inner + term
                probs.append(part)
                grad_probs.append(grad_part)
                value_sum[b] += rows_inner(part.astype(BF), own_grad)
            out = None
            for b in range(sources):
                grad_scores = (probs[b] * (grad_probs[b] - inner)).astype(BF)
                term = times(grad_scores, mixed_ref[b, 0, :, LANES : 2 * LANES])
                out = term if out is None else out + term
                key_sum[b] += rows_inner(grad_scores, own)
            outs.append(out)
        out_ref[a, 0, :, 0:LANES] = (jnp.where(low_lanes, outs[0], outs[1]) * SCALE).astype(BF)
        return carry

    lax.fori_loop(0, sources, one_source, 0)
    for b in range(sources):
        out_ref[b, 0, :, LANES : 2 * LANES] = (key_sum[b] * SCALE).astype(BF)
        out_ref[b, 0, :, 2 * LANES : 3 * LANES] = value_sum[b].astype(BF)


def attention_specs(sources, slot, width):
    return pl.BlockSpec((sources, 1, slot, width), lambda i, p: (0, i, 0, p))


def attend_forward(counts, mixed):
    sources, images, slot, width = mixed.shape
    pairs = width // (3 * LANES)
    work = 4 * images * pairs * (sources * slot) ** 2 * LANES
    return pl.pallas_call(
        forward_kernel,
        grid=(images, pairs),
        in_specs=[
            pl.BlockSpec(memory_space=pltpu.SMEM),
            attention_specs(sources, slot, 3 * LANES),
        ],
        out_specs=attention_specs(sources, slot, LANES),
        out_shape=jax.ShapeDtypeStruct((sources, images, slot, pairs * LANES), BF),
        compiler_params=pltpu.CompilerParams(vmem_limit_bytes=40 * 2**20),
        cost_estimate=pl.CostEstimate(flops=work, bytes_accessed=mixed.size * 3, transcendentals=0),
    )(counts, mixed)


def attend_backward(counts, mixed, grad_attended):
    sources, images, slot, width = mixed.shape
    pairs = width // (3 * LANES)
    work = 10 * images * pairs * (sources * slot) ** 2 * LANES
    return pl.pallas_call(
        backward_kernel,
        grid=(images, pairs),
        in_specs=[
            pl.BlockSpec(memory_space=pltpu.SMEM),
            attention_specs(sources, slot, 3 * LANES),
            attention_specs(sources, slot, LANES),
        ],
        out_specs=attention_specs(sources, slot, 3 * LANES),
        out_shape=jax.ShapeDtypeStruct(mixed.shape, BF),
        scratch_shapes=[
            pltpu.VMEM((sources, slot, LANES), F32),
            pltpu.VMEM((sources, slot, LANES), F32),
        ],
        compiler_params=pltpu.CompilerParams(vmem_limit_bytes=40 * 2**20),
        cost_estimate=pl.CostEstimate(flops=work, bytes_accessed=mixed.size * 5, transcendentals=0),
    )(counts, mixed, grad_attended)


def flip(values, offset):
    perm = [(rank, rank ^ offset) for rank in range(lax.axis_size("shard"))]
    return lax.ppermute(values, "shard", perm)


def gather_weight(weight):
    shards, rank, core = lax.axis_size("shard"), lax.axis_index("shard"), lax.axis_index("core")
    rows, columns = weight.shape
    halves = weight.reshape(2, rows // 2, columns)
    mine = lax.dynamic_index_in_dim(halves, core, 0, keepdims=False)
    full = jnp.zeros((shards, 2, rows // 2, columns), weight.dtype)
    full = lax.dynamic_update_slice(full, halves[None], (rank, 0, 0, 0))
    for offset in range(1, shards):
        piece = flip(mine, offset)
        partner = lax.ppermute(piece, "core", SWAP)
        owner = rank ^ offset
        full = lax.dynamic_update_slice(full, piece[None, None], (owner, core, 0, 0))
        full = lax.dynamic_update_slice(full, partner[None, None], (owner, 1 - core, 0, 0))
    return full.reshape(shards * rows, columns)


def reduce_weight(grad):
    shards, rank, core = lax.axis_size("shard"), lax.axis_index("shard"), lax.axis_index("core")
    rows, columns = grad.shape
    halves = grad.reshape(shards, 2, rows // shards // 2, columns)
    own = lax.dynamic_index_in_dim(halves, core, 1, keepdims=False)
    other = lax.dynamic_index_in_dim(halves, 1 - core, 1, keepdims=False).astype(BF)
    received = lax.ppermute(other, "core", SWAP)
    chip = (own + received.astype(F32)).astype(BF)
    group = lax.dynamic_index_in_dim(chip, rank, 0, keepdims=False).astype(F32)
    for offset in range(1, shards):
        piece = lax.dynamic_index_in_dim(chip, rank ^ offset, 0, keepdims=False)
        group = group + flip(piece, offset).astype(F32)
    part = lax.psum_scatter(group.astype(BF), "rep", scatter_dimension=0, tiled=True)
    total = lax.all_gather(part, "rep", axis=0, tiled=True)
    partner = lax.ppermute(total, "core", SWAP)
    pair = jnp.stack([jnp.where(core == 0, total, partner), jnp.where(core == 0, partner, total)])
    return pair.reshape(rows // shards, columns).astype(F32)


def columns_to_heads(values):
    shards, rank = lax.axis_size("shard"), lax.axis_index("shard")
    wide = values.shape[1] // shards
    pieces = []
    for offset in range(shards):
        piece = lax.dynamic_slice_in_dim(values, (rank ^ offset) * wide, wide, 1)
        pieces.append(flip(piece, offset) if offset else piece)
    return jnp.stack(pieces)


def heads_to_columns(stacked):
    shards, rank = lax.axis_size("shard"), lax.axis_index("shard")
    wide = stacked.shape[2]
    full = jnp.zeros((stacked.shape[1], shards * wide), stacked.dtype)
    for offset in range(shards):
        piece = flip(stacked[offset], offset) if offset else stacked[0]
        full = lax.dynamic_update_slice(full, piece, (0, (rank ^ offset) * wide))
    return full


def per_device(tokens, counts, w_qkv, w_proj, w_fc1, w_fc2, norm_gains, biases, grad_out):
    images, slot_rows, width = tokens.shape
    shards = lax.axis_size("shard")
    shard_rank = lax.axis_index("shard")
    row_count = images * slot_rows
    shaped = (images, slot_rows, width)
    pairs = width // LANES
    own_counts = lax.dynamic_slice_in_dim(counts, shard_rank, 1, 1)
    slot_index = jnp.arange(slot_rows, dtype=jnp.int32)
    row_valid = (slot_index[None, :] < own_counts).astype(F32).reshape(row_count, 1)

    qkv_paired = w_qkv.reshape(-1, 3, pairs, LANES).swapaxes(1, 2).reshape(w_qkv.shape)
    vectors = lax.all_gather(jnp.concatenate([norm_gains, biases]), "shard", axis=0, tiled=False)
    gain_len = norm_gains.shape[0]
    gains_wide = vectors[:, :gain_len].reshape(-1).astype(F32)
    biases_wide = vectors[:, gain_len:].reshape(-1).astype(F32)
    qkv_full = gather_weight(qkv_paired)
    proj_full = gather_weight(w_proj)
    fc1_full = gather_weight(w_fc1)
    fc2_full = gather_weight(w_fc2)

    inputs = tokens.astype(F32).reshape(row_count, width)
    normed_wide, norm_one_back = jax.vjp(
        layer_norm, inputs, gains_wide[:width], biases_wide[:width]
    )
    normed_one = normed_wide.astype(BF)
    query_bias = biases_wide[2 * width : 3 * width].reshape(pairs, 1, LANES)
    value_bias = biases_wide[3 * width : 4 * width].reshape(pairs, 1, LANES)
    mixed_bias = jnp.concatenate([query_bias, jnp.zeros_like(query_bias), value_bias], axis=1)
    mixed = (times(normed_one, qkv_full) + mixed_bias.reshape(1, 3 * width)).astype(BF)
    own_heads = columns_to_heads(mixed).reshape(shards, images, slot_rows, -1)
    source_counts = jnp.take(counts, jnp.arange(shards) ^ shard_rank, axis=1)
    attended = attend_forward(source_counts, own_heads)
    attended = heads_to_columns(attended.reshape(shards, row_count, -1))
    middle = inputs + times(attended, proj_full) + biases_wide[4 * width : 5 * width]
    normed_mid, norm_two_back = jax.vjp(
        layer_norm, middle, gains_wide[width:], biases_wide[width : 2 * width]
    )
    normed_two = normed_mid.astype(BF)
    before = times(normed_two, fc1_full) + biases_wide[6 * width :]
    normal_cdf = 0.5 + 0.5 * lax.erf(before * 0.5**0.5)
    density = jnp.exp(-0.5 * before * before) * (2.0 * jnp.pi) ** -0.5
    hidden, gelu_slope = lax.optimization_barrier(
        ((before * normal_cdf).astype(BF), normal_cdf + before * density)
    )
    outcome = (middle + times(hidden, fc2_full) + biases_wide[5 * width : 6 * width]) * row_valid
    output = outcome.astype(BF).reshape(shaped)

    grad_rows = grad_out.astype(F32).reshape(row_count, width) * row_valid
    grad_branch = grad_rows.astype(BF)
    grad_fc2 = reduce_weight(rows_inner(hidden, grad_branch))
    grad_out_bias = jnp.sum(grad_branch, axis=0, dtype=F32)
    grad_before = (times_transpose(grad_branch, fc2_full) * gelu_slope).astype(BF)
    grad_fc1 = reduce_weight(rows_inner(normed_two, grad_before))
    grad_hidden_bias = jnp.sum(grad_before, axis=0, dtype=F32)
    grad_normed_two = times_transpose(grad_before, fc1_full)
    grad_middle_norm, grad_gain_two, grad_shift_two = norm_two_back(grad_normed_two)
    grad_middle = grad_rows + grad_middle_norm
    grad_branch_one = grad_middle.astype(BF)
    grad_proj = reduce_weight(rows_inner(attended, grad_branch_one))
    grad_proj_bias = jnp.sum(grad_branch_one, axis=0, dtype=F32)
    grad_attended = times_transpose(grad_branch_one, proj_full).astype(BF)
    grad_heads = columns_to_heads(grad_attended).reshape(shards, images, slot_rows, -1)
    grad_own = attend_backward(source_counts, own_heads, grad_heads)
    grad_mixed = heads_to_columns(grad_own.reshape(shards, row_count, -1))
    grad_qkv = reduce_weight(rows_inner(normed_one, grad_mixed))
    grad_qkv = grad_qkv.reshape(-1, pairs, 3, LANES).swapaxes(1, 2).reshape(w_qkv.shape)
    column_sums = jnp.sum(grad_mixed, axis=0, dtype=F32).reshape(pairs, 3, LANES)
    grad_normed_one = times_transpose(grad_mixed, qkv_full)
    grad_inputs_norm, grad_gain_one, grad_shift_one = norm_one_back(grad_normed_one)
    grad_tokens = (grad_middle + grad_inputs_norm).reshape(shaped)
    grad_gains = jnp.concatenate([grad_gain_one, grad_gain_two]).reshape(shards, -1)
    grad_biases = jnp.concatenate(
        [
            grad_shift_one,
            grad_shift_two,
            column_sums[:, 0].reshape(-1),
            column_sums[:, 2].reshape(-1),
            grad_proj_bias,
            grad_out_bias,
            grad_hidden_bias,
        ]
    ).reshape(shards, -1)
    grad_vectors = lax.psum(
        jnp.concatenate([grad_gains, grad_biases], axis=1), ("rep", "core", "shard")
    )
    own_vectors = lax.dynamic_index_in_dim(grad_vectors, shard_rank, 0, keepdims=False)
    return (
        output,
        grad_tokens,
        grad_qkv,
        grad_proj,
        grad_fc1,
        grad_fc2,
        own_vectors[:gain_len],
        own_vectors[gain_len:],
    )


def solution(mesh):
    replicas, shards = mesh.devices.shape
    split = Mesh(mesh.devices.reshape(replicas // 2, 2, shards), ("rep", "core", "shard"))
    both = ("rep", "core")
    rows, weight, vector = P(both, "shard", None), P("shard", None), P("shard")
    in_specs = (rows, P(both, None)) + (weight,) * 4 + (vector,) * 2 + (rows,)
    out_specs = (rows, rows) + (weight,) * 4 + (vector,) * 2
    return jax.shard_map(
        per_device, mesh=split, in_specs=in_specs, out_specs=out_specs, check_vma=False
    )
```

```python
import functools

import jax
import jax.numpy as jnp
from jax import lax
from jax.experimental import pallas as pl
from jax.experimental.pallas import tpu as pltpu
from jax.sharding import Mesh, PartitionSpec as P

HEAD = 64
LANES = 2 * HEAD
SCALE = HEAD ** (-0.5)

norm_eps = 1e-06
big_negative = -1e30
BF = jnp.bfloat16
F32 = jnp.float32
SWAP = [(0, 1), (1, 0)]


def layer_norm(values, norm_gain, norm_shift):
    centered = values - jnp.mean(values, axis=-1, keepdims=True)
    spread = jnp.mean(centered * centered, axis=-1, keepdims=True)
    return centered * lax.rsqrt(spread + norm_eps) * norm_gain + norm_shift


def rows_inner(left, right):
    return lax.dot_general(left, right, (((0,), (0,)), ((), ())), preferred_element_type=F32)


def times_transpose(left, right):
    return lax.dot_general(left, right, (((1,), (1,)), ((), ())), preferred_element_type=F32)


def times(left, right):
    return jnp.dot(left, right, preferred_element_type=F32)


def softmax_parts(query, mixed_ref, key_masks, sources):
    scores = []
    for b in range(sources):
        key_rows = mixed_ref[b, 0, :, LANES : 2 * LANES]
        scores.append(jnp.where(key_masks[b], times_transpose(query, key_rows) * SCALE, big_negative))
    row_max = functools.reduce(
        jnp.maximum, [jnp.max(part, axis=1, keepdims=True) for part in scores]
    )
    exps = [jnp.exp(part - row_max) for part in scores]
    total = functools.reduce(jnp.add, [jnp.sum(part, axis=1, keepdims=True) for part in exps])
    return exps, 1.0 / total


def masks_of(counts_ref, image, sources, slot):
    column = lax.broadcasted_iota(jnp.int32, (1, slot), 1)
    return [column < counts_ref[image, b] for b in range(sources)]


def forward_kernel(counts_ref, mixed_ref, attended_ref):
    sources, slot = mixed_ref.shape[0], mixed_ref.shape[2]
    key_masks = masks_of(counts_ref, pl.program_id(0), sources, slot)
    low_lanes = lax.broadcasted_iota(jnp.int32, (1, LANES), 1) < HEAD

    def one_source(a, carry):
        query = mixed_ref[a, 0, :, 0:LANES]
        outs = []
        for head in range(2):
            kept = low_lanes if head == 0 else jnp.logical_not(low_lanes)
            own = jnp.where(kept, query, jnp.zeros_like(query))
            exps, inverse = softmax_parts(own, mixed_ref, key_masks, sources)
            out = None
            for b in range(sources):
                probs = (exps[b] * inverse).astype(BF)
                term = times(probs, mixed_ref[b, 0, :, 2 * LANES : 3 * LANES])
                out = term if out is None else out + term
            outs.append(out)
        attended_ref[a, 0] = jnp.where(low_lanes, outs[0], outs[1]).astype(BF)
        return carry

    lax.fori_loop(0, sources, one_source, 0)


def backward_kernel(counts_ref, mixed_ref, grad_ref, out_ref, key_sum, value_sum):
    sources, slot = mixed_ref.shape[0], mixed_ref.shape[2]
    key_masks = masks_of(counts_ref, pl.program_id(0), sources, slot)
    low_lanes = lax.broadcasted_iota(jnp.int32, (1, LANES), 1) < HEAD
    key_sum[...] = jnp.zeros_like(key_sum)
    value_sum[...] = jnp.zeros_like(value_sum)

    def one_source(a, carry):
        query = mixed_ref[a, 0, :, 0:LANES]
        grad = grad_ref[a, 0]
        outs = []
        for head in range(2):
            kept = low_lanes if head == 0 else jnp.logical_not(low_lanes)
            own = jnp.where(kept, query, jnp.zeros_like(query))
            own_grad = jnp.where(kept, grad, jnp.zeros_like(grad))
            exps, inverse = softmax_parts(own, mixed_ref, key_masks, sources)
            probs, grad_probs, inner = [], [], None
            for b in range(sources):
                part = exps[b] * inverse
                grad_part = times_transpose(own_grad, mixed_ref[b, 0, :, 2 * LANES : 3 * LANES])
                term = jnp.sum(part * grad_part, axis=1, keepdims=True)
                inner = term if inner is None else inner + term
                probs.append(part)
                grad_probs.append(grad_part)
                value_sum[b] += rows_inner(part.astype(BF), own_grad)
            out = None
            for b in range(sources):
                grad_scores = (probs[b] * (grad_probs[b] - inner)).astype(BF)
                term = times(grad_scores, mixed_ref[b, 0, :, LANES : 2 * LANES])
                out = term if out is None else out + term
                key_sum[b] += rows_inner(grad_scores, own)
            outs.append(out)
        out_ref[a, 0, :, 0:LANES] = (jnp.where(low_lanes, outs[0], outs[1]) * SCALE).astype(BF)
        return carry

    lax.fori_loop(0, sources, one_source, 0)
    for b in range(sources):
        out_ref[b, 0, :, LANES : 2 * LANES] = (key_sum[b] * SCALE).astype(BF)
        out_ref[b, 0, :, 2 * LANES : 3 * LANES] = value_sum[b].astype(BF)


def attention_specs(sources, slot, width):
    return pl.BlockSpec((sources, 1, slot, width), lambda i, p: (0, i, 0, p))


def attend_forward(counts, mixed):
    sources, images, slot, width = mixed.shape
    pairs = width // (3 * LANES)
    work = 4 * images * pairs * (sources * slot) ** 2 * LANES
    return pl.pallas_call(
        forward_kernel,
        grid=(images, pairs),
        in_specs=[
            pl.BlockSpec(memory_space=pltpu.SMEM),
            attention_specs(sources, slot, 3 * LANES),
        ],
        out_specs=attention_specs(sources, slot, LANES),
        out_shape=jax.ShapeDtypeStruct((sources, images, slot, pairs * LANES), BF),
        compiler_params=pltpu.CompilerParams(vmem_limit_bytes=40 * 2**20),
        cost_estimate=pl.CostEstimate(flops=work, bytes_accessed=mixed.size * 3, transcendentals=0),
    )(counts, mixed)


def attend_backward(counts, mixed, grad_attended):
    sources, images, slot, width = mixed.shape
    pairs = width // (3 * LANES)
    work = 10 * images * pairs * (sources * slot) ** 2 * LANES
    return pl.pallas_call(
        backward_kernel,
        grid=(images, pairs),
        in_specs=[
            pl.BlockSpec(memory_space=pltpu.SMEM),
            attention_specs(sources, slot, 3 * LANES),
            attention_specs(sources, slot, LANES),
        ],
        out_specs=attention_specs(sources, slot, 3 * LANES),
        out_shape=jax.ShapeDtypeStruct(mixed.shape, BF),
        scratch_shapes=[
            pltpu.VMEM((sources, slot, LANES), F32),
            pltpu.VMEM((sources, slot, LANES), F32),
        ],
        compiler_params=pltpu.CompilerParams(vmem_limit_bytes=40 * 2**20),
        cost_estimate=pl.CostEstimate(flops=work, bytes_accessed=mixed.size * 5, transcendentals=0),
    )(counts, mixed, grad_attended)


def flip(values, offset, axis="shard"):
    perm = [(rank, rank ^ offset) for rank in range(lax.axis_size(axis))]
    return lax.ppermute(values, axis, perm)


def gather_rows(values, axis):
    ranks, rank = lax.axis_size(axis), lax.axis_index(axis)
    full = jnp.zeros((ranks,) + values.shape, values.dtype)
    origin = (0,) * values.ndim
    for offset in range(ranks):
        piece = flip(values, offset, axis) if offset else values
        full = lax.dynamic_update_slice(full, piece[None], (rank ^ offset,) + origin)
    return full


def scatter_sum(values, axis):
    ranks, rank = lax.axis_size(axis), lax.axis_index(axis)
    total = lax.dynamic_index_in_dim(values, rank, 0, keepdims=False).astype(F32)
    for offset in range(1, ranks):
        piece = lax.dynamic_index_in_dim(values, rank ^ offset, 0, keepdims=False)
        total = total + flip(piece, offset, axis).astype(F32)
    return total


def butterfly_sum(values, axis):
    offset = 1
    while offset < lax.axis_size(axis):
        values = values + flip(values, offset, axis)
        offset *= 2
    return values


def gather_weight(weight):
    shards, rank, core = lax.axis_size("shard"), lax.axis_index("shard"), lax.axis_index("core")
    rows, columns = weight.shape
    halves = weight.reshape(2, rows // 2, columns)
    mine = lax.dynamic_index_in_dim(halves, core, 0, keepdims=False)
    full = jnp.zeros((shards, 2, rows // 2, columns), weight.dtype)
    full = lax.dynamic_update_slice(full, halves[None], (rank, 0, 0, 0))
    for offset in range(1, shards):
        piece = flip(mine, offset)
        partner = lax.ppermute(piece, "core", SWAP)
        owner = rank ^ offset
        full = lax.dynamic_update_slice(full, piece[None, None], (owner, core, 0, 0))
        full = lax.dynamic_update_slice(full, partner[None, None], (owner, 1 - core, 0, 0))
    return full.reshape(shards * rows, columns)


def chip_sum(grad):
    shards, core = lax.axis_size("shard"), lax.axis_index("core")
    rows, columns = grad.shape
    halves = grad.reshape(shards, 2, rows // shards // 2, columns)
    own = lax.dynamic_index_in_dim(halves, core, 1, keepdims=False)
    other = lax.dynamic_index_in_dim(halves, 1 - core, 1, keepdims=False).astype(BF)
    received = lax.ppermute(other, "core", SWAP)
    return (own + received.astype(F32)).astype(BF)


def finish_weight(chip):
    replicas, core = lax.axis_size("rep"), lax.axis_index("core")
    rows, columns = chip.shape[1:]
    group = scatter_sum(chip, "shard").astype(BF)
    part = scatter_sum(group.reshape(replicas, rows // replicas, columns), "rep").astype(BF)
    total = gather_rows(part, "rep").reshape(rows, columns)
    partner = lax.ppermute(total, "core", SWAP)
    pair = jnp.stack([jnp.where(core == 0, total, partner), jnp.where(core == 0, partner, total)])
    return pair.reshape(2 * rows, columns).astype(F32)


def columns_to_heads(values):
    shards, rank = lax.axis_size("shard"), lax.axis_index("shard")
    wide = values.shape[1] // shards
    pieces = []
    for offset in range(shards):
        piece = lax.dynamic_slice_in_dim(values, (rank ^ offset) * wide, wide, 1)
        pieces.append(flip(piece, offset) if offset else piece)
    return jnp.stack(pieces)


def heads_to_columns(stacked):
    shards, rank = lax.axis_size("shard"), lax.axis_index("shard")
    wide = stacked.shape[2]
    full = jnp.zeros((stacked.shape[1], shards * wide), stacked.dtype)
    for offset in range(shards):
        piece = flip(stacked[offset], offset) if offset else stacked[0]
        full = lax.dynamic_update_slice(full, piece, (0, (rank ^ offset) * wide))
    return full


def per_device(tokens, counts, w_qkv, w_proj, w_fc1, w_fc2, norm_gains, biases, grad_out):
    images, slot_rows, width = tokens.shape
    shards = lax.axis_size("shard")
    shard_rank = lax.axis_index("shard")
    row_count = images * slot_rows
    shaped = (images, slot_rows, width)
    pairs = width // LANES
    own_counts = lax.dynamic_slice_in_dim(counts, shard_rank, 1, 1)
    slot_index = jnp.arange(slot_rows, dtype=jnp.int32)
    row_valid = (slot_index[None, :] < own_counts).astype(F32).reshape(row_count, 1)

    qkv_paired = w_qkv.reshape(-1, 3, pairs, LANES).swapaxes(1, 2).reshape(w_qkv.shape)
    vectors = gather_rows(jnp.concatenate([norm_gains, biases]), "shard")
    gain_len = norm_gains.shape[0]
    gains_wide = vectors[:, :gain_len].reshape(-1).astype(F32)
    biases_wide = vectors[:, gain_len:].reshape(-1).astype(F32)
    qkv_full = gather_weight(qkv_paired)

    inputs = tokens.astype(F32).reshape(row_count, width)
    normed_wide, norm_one_back = jax.vjp(
        layer_norm, inputs, gains_wide[:width], biases_wide[:width]
    )
    normed_one = normed_wide.astype(BF)
    query_bias = biases_wide[2 * width : 3 * width].reshape(pairs, 1, LANES)
    value_bias = biases_wide[3 * width : 4 * width].reshape(pairs, 1, LANES)
    mixed_bias = jnp.concatenate([query_bias, jnp.zeros_like(query_bias), value_bias], axis=1)
    mixed = (times(normed_one, qkv_full) + mixed_bias.reshape(1, 3 * width)).astype(BF)
    own_heads, w_proj, w_fc1, w_fc2 = lax.optimization_barrier(
        (columns_to_heads(mixed), w_proj, w_fc1, w_fc2)
    )
    proj_full = gather_weight(w_proj)
    fc1_full = gather_weight(w_fc1)
    fc2_full = gather_weight(w_fc2)
    own_heads = own_heads.reshape(shards, images, slot_rows, -1)
    source_counts = jnp.take(counts, jnp.arange(shards) ^ shard_rank, axis=1)
    attended = attend_forward(source_counts, own_heads)
    attended = heads_to_columns(attended.reshape(shards, row_count, -1))
    middle = inputs + times(attended, proj_full) + biases_wide[4 * width : 5 * width]
    normed_mid, norm_two_back = jax.vjp(
        layer_norm, middle, gains_wide[width:], biases_wide[width : 2 * width]
    )
    normed_two = normed_mid.astype(BF)
    before = times(normed_two, fc1_full) + biases_wide[6 * width :]
    normal_cdf = 0.5 + 0.5 * lax.erf(before * 0.5**0.5)
    density = jnp.exp(-0.5 * before * before) * (2.0 * jnp.pi) ** -0.5
    hidden, gelu_slope = lax.optimization_barrier(
        ((before * normal_cdf).astype(BF), normal_cdf + before * density)
    )
    outcome = (middle + times(hidden, fc2_full) + biases_wide[5 * width : 6 * width]) * row_valid
    output = outcome.astype(BF).reshape(shaped)

    grad_rows = grad_out.astype(F32).reshape(row_count, width) * row_valid
    grad_branch = grad_rows.astype(BF)
    chip_fc2 = chip_sum(rows_inner(hidden, grad_branch))
    grad_out_bias = jnp.sum(grad_branch, axis=0, dtype=F32)
    grad_before = (times_transpose(grad_branch, fc2_full) * gelu_slope).astype(BF)
    chip_fc1 = chip_sum(rows_inner(normed_two, grad_before))
    grad_hidden_bias = jnp.sum(grad_before, axis=0, dtype=F32)
    grad_normed_two = times_transpose(grad_before, fc1_full)
    grad_middle_norm, grad_gain_two, grad_shift_two = norm_two_back(grad_normed_two)
    grad_middle = grad_rows + grad_middle_norm
    grad_branch_one = grad_middle.astype(BF)
    chip_proj = chip_sum(rows_inner(attended, grad_branch_one))
    grad_proj_bias = jnp.sum(grad_branch_one, axis=0, dtype=F32)
    grad_attended = times_transpose(grad_branch_one, proj_full).astype(BF)
    grad_attended, chip_fc2, chip_fc1, chip_proj = lax.optimization_barrier(
        (grad_attended, chip_fc2, chip_fc1, chip_proj)
    )
    grad_fc2 = finish_weight(chip_fc2)
    grad_fc1 = finish_weight(chip_fc1)
    grad_proj = finish_weight(chip_proj)
    grad_heads = columns_to_heads(grad_attended).reshape(shards, images, slot_rows, -1)
    grad_own = attend_backward(source_counts, own_heads, grad_heads)
    grad_mixed = heads_to_columns(grad_own.reshape(shards, row_count, -1))
    grad_qkv = finish_weight(chip_sum(rows_inner(normed_one, grad_mixed)))
    grad_qkv = grad_qkv.reshape(-1, pairs, 3, LANES).swapaxes(1, 2).reshape(w_qkv.shape)
    column_sums = jnp.sum(grad_mixed, axis=0, dtype=F32).reshape(pairs, 3, LANES)
    grad_normed_one = times_transpose(grad_mixed, qkv_full)
    grad_inputs_norm, grad_gain_one, grad_shift_one = norm_one_back(grad_normed_one)
    grad_tokens = (grad_middle + grad_inputs_norm).reshape(shaped)
    grad_gains = jnp.concatenate([grad_gain_one, grad_gain_two]).reshape(shards, -1)
    grad_biases = jnp.concatenate(
        [
            grad_shift_one,
            grad_shift_two,
            column_sums[:, 0].reshape(-1),
            column_sums[:, 2].reshape(-1),
            grad_proj_bias,
            grad_out_bias,
            grad_hidden_bias,
        ]
    ).reshape(shards, -1)
    own_vectors = scatter_sum(jnp.concatenate([grad_gains, grad_biases], axis=1), "shard")
    own_vectors = butterfly_sum(butterfly_sum(own_vectors, "core"), "rep")
    return (
        output,
        grad_tokens,
        grad_qkv,
        grad_proj,
        grad_fc1,
        grad_fc2,
        own_vectors[:gain_len],
        own_vectors[gain_len:],
    )


def solution(mesh):
    replicas, shards = mesh.devices.shape
    split = Mesh(mesh.devices.reshape(replicas // 2, 2, shards), ("rep", "core", "shard"))
    both = ("rep", "core")
    rows, weight, vector = P(both, "shard", None), P("shard", None), P("shard")
    in_specs = (rows, P(both, None)) + (weight,) * 4 + (vector,) * 2 + (rows,)
    out_specs = (rows, rows) + (weight,) * 4 + (vector,) * 2
    return jax.shard_map(
        per_device, mesh=split, in_specs=in_specs, out_specs=out_specs, check_vma=False
    )
```
